768 devices in a mesh: dp: 12 (over z_lo, core), blk: 64 (over y, x, z_hi).
Axes of the slice: x: 4, y: 8, z: 12 (z_hi: 2, z_lo: 6; z = z_hi * 6 + z_lo), core: 2. Of those that a mesh axis runs over, the one named last changes fastest.
Arguments:
- held_acts: bfloat16 [565248, 768], P(('dp', 'blk')), may hold values from -24 to 24
- held_grads: bfloat16 [565248, 1536], P(('dp', 'blk')), may hold values from -6 to 6
- layer_scale: float32 [1536], replicated, may hold values from 0.25 to 4
- out_weight: bfloat16 [768, 1536], P('blk'), may hold values from -0.21875 to 0.21875
- send_slots: int32 [12, 64, 12], P('dp', 'blk'), may hold values from -1 to 22, as said below
- out_source: int32 [12, 64, 12], P('dp', 'blk'), may hold values from 0 to 34, as said below
Outputs:
- grad_acts: bfloat16 [294912, 768], P(('dp', 'blk'))
- grad_weight: float32 [768, 1536], P(('dp', 'blk'))
The draws below stay inside these ranges and needn't reach their ends.
Inputs may be any that keep to these rules, and one draw needn't show every extreme that they name: `send_slots`: for each device and each dp index e: the held block that the device passes to the device of dp index e with the same blk index, or -1 for none. A device passes nothing to itself, passed blocks are distinct, and none of them is named by the device's own out_source. `out_source`: every block passed by send_slots is named exactly once, by its receiver; no held block is named twice. Each device's blocks below 23 are its blocks 0 to k - 1 for some k, in order, followed by received blocks.
All inputs are finite; a program needn't handle non-finite values.
Results may differ from the reference program's by a relative error of at most 0.0049.
Values may be sent and summed in bfloat16 or wider, within the bound.
A program may use at most 64 MiB of HBM per device.

```python
import math
import jax
import jax.numpy as jnp
from jax import lax

D = 1536
BLOCK = 32
OUT_BLK = 12
HD_ALL = 768
HELD_BLK = 23
ROWS_DEV = 384
TOTAL_ROWS = 294912
HELD_TOTAL = 565248
N_DP = 12
N_BLK = 64


def route_group(key):
    key_mask, key_send, key_recv = jax.random.split(key, 3)
    passes = jax.random.randint(key_mask, (N_DP, N_DP), 0, 2)
    sender = jax.random.randint(key_send, (), 0, N_DP)
    receiver = (sender + 1 + jax.random.randint(key_recv, (), 0, N_DP - 1)) % N_DP
    row_ids = jnp.arange(N_DP)[:, None]
    col_ids = jnp.arange(N_DP)[None, :]
    passes = jnp.where(col_ids == sender, 0, passes)
    passes = jnp.where(row_ids == sender, 1, passes)
    passes = jnp.where(col_ids == receiver, 1, passes)
    another = jnp.where((receiver + 1) % N_DP == sender, (receiver + 2) % N_DP, (receiver + 1) % N_DP)
    forced = (receiver == N_DP - 1) & (row_ids == receiver) & (col_ids == another)
    passes = jnp.where(forced, 1, passes)
    passes = jnp.where(row_ids == col_ids, 0, passes)
    recv_count = jnp.sum(passes, axis=0)
    kept_count = OUT_BLK - recv_count
    order_rank = jnp.cumsum(passes, axis=1) - passes
    send_list = jnp.where(passes == 1, kept_count[:, None] + order_rank, -1)
    arrival = jnp.argsort((1 - passes.T) * N_DP + jnp.arange(N_DP)[None, :], axis=1)
    outputs = jnp.arange(OUT_BLK)[None, :]
    slot_pick = jnp.clip(outputs - kept_count[:, None], 0, N_DP - 1)
    source_list = jnp.where(outputs < kept_count[:, None], outputs, HELD_BLK + jnp.take_along_axis(arrival, slot_pick, axis=1))
    return (send_list.astype(jnp.int32), source_list.astype(jnp.int32))


def routing(key):
    group_keys = jax.random.split(key, N_BLK)
    send_list, source_list = jax.vmap(route_group)(group_keys)
    return (jnp.transpose(send_list, (1, 0, 2)), jnp.transpose(source_list, (1, 0, 2)))


def draw_send_slots(key, part):
    return routing(key)[0]


def draw_out_source(key, part):
    return routing(key)[1]


def strengthened(entries, own_key, source, target, parts, factor):
    def block_of(axis_at):
        return (jnp.arange(entries.shape[axis_at]) // (entries.shape[axis_at] // parts)).reshape((-1,) + (1,) * (entries.ndim - 1 - axis_at))

    first = jax.random.permutation(own_key, parts)[block_of(target)]
    far = (block_of(target) + parts // 2) % parts
    return jnp.where((block_of(source) == first) | (block_of(source) == far), factor * entries, entries)


def level_of(rng, extent, cuts, smallest, largest):
    gain, own = 1.0, jax.random.fold_in(rng, 6)
    for dim, shards_of in cuts:
        heights = jnp.exp(jax.random.uniform(jax.random.fold_in(own, dim), (shards_of,), jnp.float32, smallest / len(cuts), largest / len(cuts)))
        gain = gain * jnp.repeat(heights, extent[dim] // shards_of).reshape([-1 if axis == dim else 1 for axis in range(len(extent))])
    return gain


def gaussian(rng, shape, deviation, limit, cuts=(), kind=jnp.bfloat16):
    factor_of = level_of(rng, shape, cuts, -0.22, 0.18) if cuts else 1.0
    array = jax.random.normal(rng, shape, jnp.float32) * deviation * factor_of
    return jnp.minimum(jnp.maximum(array, -limit), limit).astype(kind)


def noise_with(own_key, extent, spread, limit, cuts, heavy, kind=jnp.bfloat16):
    array = spread * jax.random.normal(own_key, extent, jnp.float32)
    if cuts:
        array = array * level_of(own_key, extent, cuts, -0.22, 0.18)
    return jnp.clip(strengthened(array, jax.random.fold_in(own_key, 3), *heavy), -limit, limit).astype(kind)


def setup_inputs(seed: int = 0) -> dict:
    splits = jax.random.split(jax.random.key(seed), 7)
    return {
        "held_acts": noise_with(splits[0], (HELD_TOTAL, HD_ALL), 1.0, 24.0, ((0, 768),), (0, 1, 768, 6.0)),
        "held_grads": gaussian(splits[1], (HELD_TOTAL, D), 1.0, 6.0, ((0, 768),)),
        "layer_scale": jnp.clip(jnp.exp(jax.random.uniform(splits[2], (D,), jnp.float32, math.log(0.25), math.log(4.0))), 0.25, 4.0),
        "out_weight": gaussian(splits[3], (HD_ALL, D), HD_ALL ** -0.5, 0.21875, ((0, 64),)),
        "send_slots": draw_send_slots(jax.random.fold_in(splits[6], 71), 0),
        "out_source": draw_out_source(jax.random.fold_in(splits[6], 71), 0),
    }


def reference(held_acts, held_grads, layer_scale, out_weight, send_slots, out_source):
    dp_ids = jnp.arange(N_DP).astype(jnp.int32)[:, None, None]
    blk_ids = jnp.arange(N_BLK).astype(jnp.int32)[None, :, None]
    is_local = out_source < HELD_BLK
    peer_index = jnp.clip(out_source - HELD_BLK, 0, N_DP - 1).astype(jnp.int32)
    sent_block = send_slots[peer_index, blk_ids, dp_ids]
    own_block = (dp_ids * N_BLK + blk_ids) * HELD_BLK + out_source
    far_block = (peer_index * N_BLK + blk_ids) * HELD_BLK + sent_block
    blocks = jnp.where(is_local, own_block, far_block).astype(jnp.int32).reshape(N_DP * N_BLK, OUT_BLK)
    offsets = jnp.arange(BLOCK).astype(jnp.int32)
    row_ids = (blocks[:, :, None] * BLOCK + offsets[None, None, :]).reshape(N_DP * N_BLK, ROWS_DEV).astype(jnp.int32)

    def accumulate(carried, device_rows):
        act_rows = held_acts[device_rows]
        grad_rows = held_grads[device_rows]
        scaled = (layer_scale[None, :] * grad_rows.astype(jnp.float32)).astype(jnp.bfloat16)
        grad_out = jnp.dot(scaled, out_weight.T, preferred_element_type=jnp.float32).astype(jnp.bfloat16)
        carried = carried + jnp.dot(act_rows.T, scaled, preferred_element_type=jnp.float32)
        return (carried, grad_out)
    summed, grad_parts = lax.scan(accumulate, jnp.zeros((HD_ALL, D), jnp.float32), row_ids)
    grad_acts = grad_parts.reshape(TOTAL_ROWS, HD_ALL)
    grad_weight = summed / math.sqrt(TOTAL_ROWS)
    return (grad_acts, grad_weight)
```

```python
import math

import jax
import jax.numpy as jnp
import ml_dtypes
import numpy as np
from jax import lax
from jax.experimental import pallas as pl
from jax.experimental.pallas import tpu as pltpu
from jax.sharding import PartitionSpec as P

MESH = pl.DeviceIdType.MESH
BF16 = jnp.bfloat16
F32 = jnp.float32
BLOCK = 32
NX, NY, NH, NL, NC = 4, 8, 2, 6, 2
NZ = NH * NL
NDP = NL * NC
HELD, OUT = 23, 12
HD, D = 768, 1536
WROWS = 12
TOTAL_ROWS = NDP * NX * NY * NH * OUT * BLOCK
GROUP = HD // NC // NX


def selection(rows, cols, pairs):
    m = np.zeros((rows, cols), np.float32)
    for r, c in pairs:
        m[r, c] = 1.0
    return m.astype(ml_dtypes.bfloat16)


def tables():
    grad_order = [
        (((c * NX + x) * NY + y) * NZ + h * NL + l, (l * NC + c) * 64 + (y * NX + x) * NH + h)
        for c in range(NC) for x in range(NX) for y in range(NY) for h in range(NH) for l in range(NL)
    ]
    weight_rows = [(WROWS * g + i, 16 * g + i) for g in range(NX * NH) for i in range(WROWS)]
    to_y = [((y * 4 + q) * NZ + z, (q * NY + y) * NZ + z) for q in range(4) for y in range(NY) for z in range(NZ)]
    to_z = [(z * 16 + 3 * q + j, (j * 4 + q) * NZ + z) for j in range(3) for q in range(4) for z in range(NZ)]
    return (
        selection(HD, HD, grad_order),
        selection(GROUP, 16 * NX * NH, weight_rows),
        selection(384, 384, to_y),
        selection(NZ * 16, 256, to_z),
    )


def matmul(a, b, dims=((1,), (0,))):
    return lax.dot_general(a, b, (dims, ((), ())), preferred_element_type=F32)


def kernel(
    acts_hbm, grads_hbm, order_hbm, scale_ref, w_ref, send_ref, source_ref, wsel_ref, ysel_ref, zsel_ref,
    ga_ref, gw_ref,
    acts, grads, order, scaled, acts_t, p_own, p_sib, p_rec, wbuf, wfull,
    xa, xd, xb, ra, rd, rb, ysend, yrecv, zsend, zrecv, gall, sbuf, rbuf,
    load_sem, wh_s, wh_r, wx_s, wx_r, ring_s, ring_r, sib_s, sib_r, pc_s, pc_r, x_s, x_r, y_s, y_r, z_s, z_r, e_s, e_r,
):
    dp = lax.axis_index("dp")
    blk = lax.axis_index("blk")
    zl, core = dp // 2, dp % 2
    y, x, zh = blk // 8, (blk // 2) % 4, blk % 2
    z = zh * NL + zl
    s = 1 - 2 * core

    def at_x(v):
        return (dp, y * 8 + v * 2 + zh)

    def at_y(v):
        return (dp, v * 8 + x * 2 + zh)

    def at_z(v):
        return ((v % NL) * 2 + core, y * 8 + x * 2 + v // NL)

    sibling = (dp + s, blk)
    z_pair = (dp, blk + 1 - 2 * zh)

    def remote(src, dst, ss, rs, dev):
        return pltpu.make_async_remote_copy(
            src_ref=src, dst_ref=dst, send_sem=ss, recv_sem=rs, device_id=dev, device_id_type=MESH
        )

    loads = [
        pltpu.make_async_copy(grads_hbm, grads, load_sem.at[0]),
        pltpu.make_async_copy(acts_hbm, acts.at[pl.ds(0, HELD * BLOCK)], load_sem.at[1]),
        pltpu.make_async_copy(order_hbm, order, load_sem.at[2]),
    ]
    for c in loads:
        c.start()

    barrier = pltpu.get_barrier_semaphore()
    peers = [at_x((x + k) % NX) for k in range(1, NX)]
    peers += [at_y((y + k) % NY) for k in range(1, NY)]
    peers += [at_z((z + k) % NZ) for k in range(1, NZ)]
    peers += [((dp + k - core + 1 - core) % NDP, blk) for k in range(0, NDP, 2)]
    for dev in peers:
        pl.semaphore_signal(barrier, inc=1, device_id=dev, device_id_type=MESH)

    half = pl.ds(pl.multiple_of(core * 768, 768), 768)
    mine = w_ref[:, half].astype(F32)
    wbuf[x, zh] = jnp.concatenate([mine, jnp.zeros((16 - WROWS, 768), F32)], 0).astype(BF16)
    acts[pl.ds(HELD * BLOCK, BLOCK), :] = jnp.zeros((BLOCK, HD), BF16)
    scaled[pl.ds(HELD * BLOCK, BLOCK), :] = jnp.zeros((BLOCK, D), BF16)
    rbuf[dp] = jnp.zeros((BLOCK, HD), BF16)

    pl.semaphore_wait(barrier, len(peers))

    wh = remote(wbuf.at[x, zh], wbuf.at[x, zh], wh_s, wh_r, z_pair)
    wh.start()

    kept = jnp.int32(0)
    for o in range(OUT):
        kept = kept + jnp.where(source_ref[o] < HELD, 1, 0)
    loads[0].wait()
    scale = scale_ref[...]

    def scale_block(j, _):
        used = j < kept
        for e in range(NDP):
            used = used | (send_ref[e] == j)
        factor = jnp.where(used, 1.0, 0.0).astype(F32)
        rows = pl.ds(pl.multiple_of(j * BLOCK, BLOCK), BLOCK)
        scaled[rows, :] = (grads[rows, :].astype(F32) * (scale * factor)).astype(BF16)
        return 0

    lax.fori_loop(0, HELD, scale_block, 0)

    remote(wbuf.at[x, 1 - zh], wbuf.at[x, 1 - zh], wh_s, wh_r, z_pair).wait_recv()
    wx = [remote(wbuf.at[x], wbuf.at[x], wx_s.at[k], wx_r.at[k], at_x((x + k) % NX)) for k in range(1, NX)]
    for c in wx:
        c.start()

    loads[1].wait()
    loads[2].wait()

    def transpose_tile(i, _):
        rows = pl.ds(pl.multiple_of(i * 384, 384), 384)
        acts_t[i] = matmul(order[rows, :], acts[...], ((1,), (1,))).astype(BF16)
        return 0

    lax.fori_loop(0, 2, transpose_tile, 0)

    for k in range(1, NX):
        v = (x - k + NX) % NX
        remote(wbuf.at[v], wbuf.at[v], wx_s.at[k], wx_r.at[k], at_x(v)).wait_recv()

    def wchunk(c, v):
        return wfull.at[c, pl.ds(pl.multiple_of(v * GROUP, GROUP), GROUP)]

    wfull[core, pl.ds(pl.multiple_of(y * GROUP, GROUP), GROUP), :] = matmul(
        wsel_ref[...], wbuf[...].reshape(16 * NX * NH, 768)
    ).astype(BF16)

    def hop(way, k):
        sign = s if way == 0 else -s
        v = (y - sign * k + 2 * NY) % NY
        sem = way * 4 + k
        return remote(wchunk(core, v), wchunk(core, v), ring_s.at[sem], ring_r.at[sem], at_y((y + sign + NY) % NY))

    def arrived(way, k):
        sign = s if way == 0 else -s
        v = (y - sign * (k + 1) + 2 * NY) % NY
        sem = way * 4 + k
        remote(wchunk(core, v), wchunk(core, v), ring_s.at[sem], ring_r.at[sem], at_y(v)).wait_recv()
        return v

    def share(v):
        j = (v - y + NY) % NY
        c = remote(wchunk(core, v), wchunk(core, v), sib_s.at[j], sib_r.at[j], sibling)
        c.start()
        return c

    hops = [hop(0, 0), hop(1, 0)]
    for c in hops:
        c.start()
    shares = [share(y)]

    def advance(k):
        for way, steps in ((0, 4), (1, 3)):
            if k < steps:
                v = arrived(way, k)
                if k + 1 < steps:
                    c = hop(way, k + 1)
                    c.start()
                    hops.append(c)
                shares.append(share(v))

    def term_tile(n, _):
        cols = pl.ds(pl.multiple_of(n * 512, 512), 512)
        t = matmul(acts_t[1 - core], scaled[:, cols]).astype(BF16)
        p_sib[:, :, cols] = t.reshape(NX, GROUP, 512)
        return 0

    lax.fori_loop(0, 3, term_tile, 0)
    order_x = [(x + 2) % NX, (x + s + NX) % NX, (x - s + NX) % NX, x]
    pc = [remote(p_sib.at[v], p_rec.at[v], pc_s.at[k], pc_r.at[k], sibling) for k, v in enumerate(order_x)]
    for c in pc:
        c.start()

    def own_tile(n, _):
        cols = pl.ds(pl.multiple_of(n * 512, 512), 512)
        t = matmul(acts_t[core], scaled[:, cols])
        p_own[:, :, cols] = t.reshape(NX, GROUP, 512)
        return 0

    lax.fori_loop(0, 3, own_tile, 0)

    right, left, far = (x + s + NX) % NX, (x - s + NX) % NX, (x + 2) % NX

    def from_sibling(k, v):
        remote(p_sib.at[v], p_rec.at[v], pc_s.at[k], pc_r.at[k], sibling).wait_recv()
        return p_own[v] + p_rec[v].astype(F32)

    advance(0)
    xa[...] = from_sibling(0, far).astype(BF16)
    ca = remote(xa, ra, x_s.at[0], x_r.at[0], at_x(right))
    ca.start()
    xd[...] = from_sibling(1, left).astype(BF16)
    cd = remote(xd, rd, x_s.at[1], x_r.at[1], at_x(left))
    cd.start()
    advance(1)
    to_right = from_sibling(2, right)
    ca.wait_recv()
    xb[...] = (to_right + ra[...].astype(F32)).astype(BF16)
    cb = remote(xb, rb, x_s.at[2], x_r.at[2], at_x(right))
    cb.start()
    advance(2)
    advance(3)

    for j in range(NY):
        v = (y + j) % NY
        remote(wchunk(1 - core, v), wchunk(1 - core, v), sib_s.at[j], sib_r.at[j], sibling).wait_recv()

    def ga_tile(i, _):
        rows = pl.ds(pl.multiple_of(i * 256, 256), 256)
        t = matmul(scaled[rows, pl.ds(0, 768)], wfull[0], ((1,), (1,)))
        t = t + matmul(scaled[rows, pl.ds(768, 768)], wfull[1], ((1,), (1,)))
        gall[pl.ds(pl.multiple_of(i * 8, 8), 8)] = t.astype(BF16).reshape(8, BLOCK, HD)
        return 0

    lax.fori_loop(0, 3, ga_tile, 0)

    ex = []
    for k in range(1, NDP):
        e = (dp + k) % NDP
        sbuf[k] = gall[jnp.maximum(send_ref[e], 0)]
        c = remote(sbuf.at[k], rbuf.at[dp], e_s.at[k], e_r.at[k], (e, blk))
        c.start()
        ex.append(c)

    mine_x = from_sibling(3, x)
    cd.wait_recv()
    cb.wait_recv()
    t = (mine_x + rd[...].astype(F32) + rb[...].astype(F32)).astype(BF16)
    stacked = jnp.concatenate([t[:, 384 * q : 384 * (q + 1)] for q in range(4)], 0)
    ysend[...] = matmul(ysel_ref[...], stacked).astype(BF16).reshape(NY, 48, 384)
    cy = []
    for k in range(1, NY):
        v = (y + k) % NY
        c = remote(ysend.at[v], yrecv.at[k], y_s.at[k], y_r.at[k], at_y(v))
        c.start()
        cy.append(c)
    total = ysend[y].astype(F32)
    for k in range(1, NY):
        cy[k - 1].wait_recv()
        total = total + yrecv[k].astype(F32)

    tz = total.astype(BF16)
    stacked = jnp.concatenate([tz[:, 128 * j : 128 * (j + 1)] for j in range(3)] + [jnp.zeros((112, 128), BF16)], 0)
    zsend[...] = matmul(zsel_ref[...], stacked).astype(BF16).reshape(NZ, 16, 128)
    cz = []
    for k in range(1, NZ):
        v = (z + k) % NZ
        c = remote(zsend.at[v], zrecv.at[k], z_s.at[k], z_r.at[k], at_z(v))
        c.start()
        cz.append(c)
    total = zsend[z].astype(F32)
    for k in range(1, NZ):
        cz[k - 1].wait_recv()
        total = total + zrecv[k].astype(F32)
    total = total / math.sqrt(TOTAL_ROWS)
    for g in range(12):
        gw_ref[:, pl.ds(128 * g, 128)] = total[g : g + 1, :]

    for c in ex:
        c.wait_recv()
    for o in range(OUT):
        v = source_ref[o]
        local = gall[jnp.minimum(v, HELD - 1)]
        got = rbuf[jnp.maximum(v - HELD, 0)]
        ga_ref[pl.ds(o * BLOCK, BLOCK), :] = jnp.where(v < HELD, local, got)

    for c in [wh, *wx, *hops, *shares, *pc, ca, cd, cb, *cy, *cz, *ex]:
        c.wait_send()


def on_device(held_acts, held_grads, layer_scale, out_weight, send_slots, out_source):
    order, wsel, ysel, zsel = (jnp.asarray(t) for t in tables())
    hbm = pl.BlockSpec(memory_space=pl.ANY)
    vmem = pl.BlockSpec(memory_space=pltpu.VMEM)
    smem = pl.BlockSpec(memory_space=pltpu.SMEM)
    dma = pltpu.SemaphoreType.DMA
    grad_acts, grad_weight = pl.pallas_call(
        kernel,
        out_shape=(
            jax.ShapeDtypeStruct((OUT * BLOCK, HD), BF16),
            jax.ShapeDtypeStruct((1, D), F32),
        ),
        in_specs=[hbm, hbm, hbm, vmem, vmem, smem, smem, vmem, vmem, vmem],
        out_specs=(vmem, vmem),
        scratch_shapes=[
            pltpu.VMEM((HD, HD), BF16),
            pltpu.VMEM((HELD * BLOCK, D), BF16),
            pltpu.VMEM((HD, HD), BF16),
            pltpu.VMEM((HD, D), BF16),
            pltpu.VMEM((NC, HD // NC, HD), BF16),
            pltpu.VMEM((NX, GROUP, D), F32),
            pltpu.VMEM((NX, GROUP, D), BF16),
            pltpu.VMEM((NX, GROUP, D), BF16),
            pltpu.VMEM((NX, NH, 16, 768), BF16),
            pltpu.VMEM((2, HD, 768), BF16),
            *[pltpu.VMEM((GROUP, D), BF16)] * 6,
            pltpu.VMEM((NY, 48, 384), BF16),
            pltpu.VMEM((NY, 48, 384), BF16),
            pltpu.VMEM((NZ, 16, 128), BF16),
            pltpu.VMEM((NZ, 16, 128), BF16),
            pltpu.VMEM((HELD + 1, BLOCK, HD), BF16),
            pltpu.VMEM((NDP, BLOCK, HD), BF16),
            pltpu.VMEM((NDP, BLOCK, HD), BF16),
            dma((3,)),
            dma, dma,
            dma((NX,)), dma((NX,)),
            dma((8,)), dma((8,)),
            dma((8,)), dma((8,)),
            dma((4,)), dma((4,)),
            dma((3,)), dma((3,)),
            dma((NY,)), dma((NY,)),
            dma((NZ,)), dma((NZ,)),
            dma((NDP,)), dma((NDP,)),
        ],
        compiler_params=pltpu.CompilerParams(
            collective_id=0, has_side_effects=True, vmem_limit_bytes=48 * 1024 * 1024
        ),
        cost_estimate=pl.CostEstimate(flops=5_000_000_000, bytes_accessed=8_000_000, transcendentals=0),
    )(
        held_acts,
        held_grads,
        order,
        layer_scale.reshape(1, D),
        out_weight,
        send_slots.reshape(NDP),
        out_source.reshape(OUT),
        wsel,
        ysel,
        zsel,
    )
    return grad_acts, grad_weight


def solution(mesh):
    in_specs = (
        P(("dp", "blk"), None),
        P(("dp", "blk"), None),
        P(),
        P("blk", None),
        P("dp", "blk", None),
        P("dp", "blk", None),
    )
    out_specs = (P(("dp", "blk"), None), P(("dp", "blk"), None))
    return jax.shard_map(
        on_device, mesh=mesh, in_specs=in_specs, out_specs=out_specs, check_vma=False
    )
```

```python
import math

import jax
import jax.numpy as jnp
import ml_dtypes
import numpy as np
from jax import lax
from jax.experimental import pallas as pl
from jax.experimental.pallas import tpu as pltpu
from jax.sharding import PartitionSpec as P

MESH = pl.DeviceIdType.MESH
BF16 = jnp.bfloat16
F32 = jnp.float32
BLOCK = 32
NX, NY, NH, NL, NC = 4, 8, 2, 6, 2
NZ = NH * NL
NDP = NL * NC
HELD, OUT = 23, 12
HD, D = 768, 1536
WROWS = 12
TOTAL_ROWS = NDP * NX * NY * NH * OUT * BLOCK
GROUP = HD // NC // NX
PIECES = 3
PIECE = GROUP // PIECES
EARLY = (6, 5, 7, 4, 8)
LATE = (3, 9, 2, 10, 1, 11)


def selection(rows, cols, pairs):
    m = np.zeros((rows, cols), np.float32)
    for r, c in pairs:
        m[r, c] = 1.0
    return m.astype(ml_dtypes.bfloat16)


def tables():
    grad_order = [
        (((c * NX + x) * NY + y) * NZ + h * NL + l, (l * NC + c) * 64 + (y * NX + x) * NH + h)
        for c in range(NC) for x in range(NX) for y in range(NY) for h in range(NH) for l in range(NL)
    ]
    weight_rows = [(WROWS * g + i, 16 * g + i) for g in range(NX * NH) for i in range(WROWS)]
    to_y = [((y * 4 + q) * NZ + z, (q * NY + y) * NZ + z) for q in range(4) for y in range(NY) for z in range(NZ)]
    to_z = [(z * 16 + 3 * q + j, (j * 4 + q) * NZ + z) for j in range(3) for q in range(4) for z in range(NZ)]
    return (
        selection(HD, HD, grad_order),
        selection(GROUP, 16 * NX * NH, weight_rows),
        selection(384, 384, to_y),
        selection(NZ * 16, 256, to_z),
    )


def matmul(a, b, dims=((1,), (0,))):
    return lax.dot_general(a, b, (dims, ((), ())), preferred_element_type=F32)


def kernel(
    acts_hbm, grads_hbm, order_hbm, scale_ref, w_ref, send_ref, source_ref, wsel_ref, ysel_ref, zsel_ref,
    ga_ref, gw_ref,
    acts, grads, order, scaled, acts_t, p_own, p_sib, p_rec, wbuf, wfull,
    xa, xd, xb, ra, rd, rb, ysend, yrecv, zsend, zrecv, gall, sbuf, rbuf, s_early, r_early, s_late,
    load_sem, wh_s, wh_r, wx_s, wx_r, ring_s, ring_r, sib_s, sib_r, pc_s, pc_r, x_s, x_r, y_s, y_r, z_s, z_r, e_s, e_r,
):
    dp = lax.axis_index("dp")
    blk = lax.axis_index("blk")
    zl, core = dp // 2, dp % 2
    y, x, zh = blk // 8, (blk // 2) % 4, blk % 2
    z = zh * NL + zl
    s = 1 - 2 * core

    def at_x(v):
        return (dp, y * 8 + v * 2 + zh)

    def at_y(v):
        return (dp, v * 8 + x * 2 + zh)

    def at_z(v):
        return ((v % NL) * 2 + core, y * 8 + x * 2 + v // NL)

    sibling = (dp + s, blk)

    def remote(src, dst, ss, rs, dev):
        return pltpu.make_async_remote_copy(
            src_ref=src, dst_ref=dst, send_sem=ss, recv_sem=rs, device_id=dev, device_id_type=MESH
        )

    loads = [
        pltpu.make_async_copy(grads_hbm, grads, load_sem.at[0]),
        pltpu.make_async_copy(acts_hbm, acts.at[pl.ds(0, HELD * BLOCK)], load_sem.at[1]),
        pltpu.make_async_copy(order_hbm, order, load_sem.at[2]),
    ]
    for c in loads:
        c.start()

    barrier = pltpu.get_barrier_semaphore()
    peers = [at_x((x + k) % NX) for k in range(1, NX)]
    peers += [at_y((y + k) % NY) for k in range(1, NY)]
    peers += [at_z((z + k) % NZ) for k in range(1, NZ)]
    peers += [((dp + k - core + 1 - core) % NDP, blk) for k in range(0, NDP, 2)]
    for dev in peers:
        pl.semaphore_signal(barrier, inc=1, device_id=dev, device_id_type=MESH)

    half = pl.ds(pl.multiple_of(core * 768, 768), 768)
    mine = w_ref[:, half].astype(F32)
    wbuf[x, zh] = jnp.concatenate([mine, jnp.zeros((16 - WROWS, 768), F32)], 0).astype(BF16)
    acts[pl.ds(HELD * BLOCK, BLOCK), :] = jnp.zeros((BLOCK, HD), BF16)
    scaled[HELD] = jnp.zeros((BLOCK, D), BF16)
    rbuf[dp] = jnp.zeros((BLOCK, HD), BF16)

    pl.semaphore_wait(barrier, len(peers))

    at_end = (zl == 0) | (zl == NL - 1)
    first = jnp.where(zl == 0, 3, 0)
    wh = [
        remote(wbuf.at[x, zh], wbuf.at[x, zh], wh_s.at[i], wh_r, at_z((1 - zh) * NL + first + i))
        for i in range(3)
    ]

    @pl.when(at_end)
    def _():
        for c in wh:
            c.start()

    kept = jnp.int32(0)
    for o in range(OUT):
        kept = kept + jnp.where(source_ref[o] < HELD, 1, 0)
    loads[0].wait()
    scale = scale_ref[...]

    def scale_block(j, _):
        used = j < kept
        for e in range(NDP):
            used = used | (send_ref[e] == j)
        factor = jnp.where(used, 1.0, 0.0).astype(F32)
        rows = pl.ds(pl.multiple_of(j * BLOCK, BLOCK), BLOCK)
        scaled[j] = (grads[rows, :].astype(F32) * (scale * factor)).astype(BF16)
        return 0

    lax.fori_loop(0, HELD, scale_block, 0)

    def chosen(k):
        return jnp.maximum(send_ref[(dp + k) % NDP], 0)

    ex = []
    for i, k in enumerate(EARLY):
        s_early[i] = scaled[chosen(k)]
        c = remote(s_early.at[i], r_early.at[i], e_s.at[k], e_r.at[k], ((dp + k) % NDP, blk))
        c.start()
        ex.append(c)

    remote(wbuf.at[x, 1 - zh], wbuf.at[x, 1 - zh], wh_s.at[0], wh_r, sibling).wait_recv()
    wx = [remote(wbuf.at[x], wbuf.at[x], wx_s.at[k], wx_r.at[k], at_x((x + k) % NX)) for k in range(1, NX)]
    for c in wx:
        c.start()

    loads[1].wait()
    loads[2].wait()

    def transpose_tile(i, _):
        rows = pl.ds(pl.multiple_of(i * 384, 384), 384)
        acts_t[i] = matmul(order[rows, :], acts[...], ((1,), (1,))).astype(BF16)
        return 0

    lax.fori_loop(0, 2, transpose_tile, 0)

    def columns(n):
        return pl.ds(pl.multiple_of(n * 512, 512), 512)

    def rows_of(n):
        return scaled[:, :, columns(n)].reshape(HD, 512)

    def term_tile(n, _):
        t = matmul(acts_t[1 - core], rows_of(n)).astype(BF16)
        p_sib[:, :, columns(n)] = t.reshape(NX, GROUP, 512)
        return 0

    lax.fori_loop(0, 3, term_tile, 0)
    order_x = [(x + 2) % NX, (x + s + NX) % NX, (x - s + NX) % NX, x]
    pc = [remote(p_sib.at[v], p_rec.at[v], pc_s.at[k], pc_r.at[k], sibling) for k, v in enumerate(order_x)]
    for c in pc:
        c.start()

    for k in range(1, NX):
        v = (x - k + NX) % NX
        remote(wbuf.at[v], wbuf.at[v], wx_s.at[k], wx_r.at[k], at_x(v)).wait_recv()

    def wchunk(c, v):
        return wfull.at[c, pl.ds(pl.multiple_of(v * GROUP, GROUP), GROUP)]

    def wpiece(v, p):
        return wfull.at[core, pl.ds(pl.multiple_of(v * GROUP + p * PIECE, PIECE), PIECE)]

    wfull[core, pl.ds(pl.multiple_of(y * GROUP, GROUP), GROUP), :] = matmul(
        wsel_ref[...], wbuf[...].reshape(16 * NX * NH, 768)
    ).astype(BF16)

    hops, shares = [], []

    def sign_of(way):
        return s if way == 0 else -s

    def hop(way, k, p):
        v = (y - sign_of(way) * k + 2 * NY) % NY
        sem = (way * 4 + k) * PIECES + p
        to = at_y((y + sign_of(way) + NY) % NY)
        c = remote(wpiece(v, p), wpiece(v, p), ring_s.at[sem], ring_r.at[sem], to)
        c.start()
        hops.append(c)

    def share(v):
        j = (v - y + NY) % NY
        c = remote(wchunk(core, v), wchunk(core, v), sib_s.at[j], sib_r.at[j], sibling)
        c.start()
        shares.append(c)

    for p in range(PIECES):
        hop(0, 0, p)
        hop(1, 0, p)
    share(y)

    def advance(k):
        for p in range(PIECES):
            for way, steps in ((0, 4), (1, 3)):
                if k < steps:
                    v = (y - sign_of(way) * (k + 1) + 2 * NY) % NY
                    sem = (way * 4 + k) * PIECES + p
                    remote(wpiece(v, p), wpiece(v, p), ring_s.at[sem], ring_r.at[sem], at_y(v)).wait_recv()
                    if k + 1 < steps:
                        hop(way, k + 1, p)
                    if p == PIECES - 1:
                        share(v)

    def own_tile(n, _):
        p_own[:, :, columns(n)] = matmul(acts_t[core], rows_of(n)).reshape(NX, GROUP, 512)
        return 0

    lax.fori_loop(0, 3, own_tile, 0)

    right, left, far = (x + s + NX) % NX, (x - s + NX) % NX, (x + 2) % NX

    def from_sibling(k, v):
        remote(p_sib.at[v], p_rec.at[v], pc_s.at[k], pc_r.at[k], sibling).wait_recv()
        return p_own[v] + p_rec[v].astype(F32)

    xa[...] = from_sibling(0, far).astype(BF16)
    ca = remote(xa, ra, x_s.at[0], x_r.at[0], at_x(right))
    ca.start()
    xd[...] = from_sibling(1, left).astype(BF16)
    cd = remote(xd, rd, x_s.at[1], x_r.at[1], at_x(left))
    cd.start()
    advance(0)
    for i, k in enumerate(LATE):
        s_late[i] = scaled[chosen(k)]
    advance(1)
    to_right = from_sibling(2, right)
    ca.wait_recv()
    xb[...] = (to_right + ra[...].astype(F32)).astype(BF16)
    cb = remote(xb, rb, x_s.at[2], x_r.at[2], at_x(right))
    cb.start()
    advance(2)
    advance(3)

    for j in range(NY):
        v = (y + j) % NY
        remote(wchunk(1 - core, v), wchunk(1 - core, v), sib_s.at[j], sib_r.at[j], sibling).wait_recv()

    def project(rows):
        t = matmul(rows[:, :768], wfull[0], ((1,), (1,)))
        t = t + matmul(rows[:, 768:], wfull[1], ((1,), (1,)))
        return t.astype(BF16)

    sbuf[...] = project(s_late[...].reshape(len(LATE) * BLOCK, D)).reshape(len(LATE), BLOCK, HD)
    for i, k in enumerate(LATE):
        c = remote(sbuf.at[i], rbuf.at[dp], e_s.at[k], e_r.at[k], ((dp + k) % NDP, blk))
        c.start()
        ex.append(c)

    def ga_tile(i, _):
        blocks = pl.ds(pl.multiple_of(i * 8, 8), 8)
        gall[blocks] = project(scaled[blocks].reshape(8 * BLOCK, D)).reshape(8, BLOCK, HD)
        return 0

    lax.fori_loop(0, 3, ga_tile, 0)

    mine_x = from_sibling(3, x)
    cd.wait_recv()
    cb.wait_recv()
    t = (mine_x + rd[...].astype(F32) + rb[...].astype(F32)).astype(BF16)
    stacked = jnp.concatenate([t[:, 384 * q : 384 * (q + 1)] for q in range(4)], 0)
    ysend[...] = matmul(ysel_ref[...], stacked).astype(BF16).reshape(NY, 48, 384)
    cy = []
    for k in range(1, NY):
        v = (y + k) % NY
        c = remote(ysend.at[v], yrecv.at[k], y_s.at[k], y_r.at[k], at_y(v))
        c.start()
        cy.append(c)
    total = ysend[y].astype(F32)
    for k in range(1, NY):
        cy[k - 1].wait_recv()
        total = total + yrecv[k].astype(F32)

    tz = total.astype(BF16)
    stacked = jnp.concatenate([tz[:, 128 * j : 128 * (j + 1)] for j in range(3)] + [jnp.zeros((112, 128), BF16)], 0)
    zsend[...] = matmul(zsel_ref[...], stacked).astype(BF16).reshape(NZ, 16, 128)
    cz = []
    for k in range(1, NZ):
        v = (z + k) % NZ
        c = remote(zsend.at[v], zrecv.at[k], z_s.at[k], z_r.at[k], at_z(v))
        c.start()
        cz.append(c)
    total = zsend[z].astype(F32)
    for k in range(1, NZ):
        cz[k - 1].wait_recv()
        total = total + zrecv[k].astype(F32)
    total = total / math.sqrt(TOTAL_ROWS)
    for g in range(12):
        gw_ref[:, pl.ds(128 * g, 128)] = total[g : g + 1, :]

    for c in ex[: len(EARLY)]:
        c.wait_recv()
    got = project(r_early[...].reshape(len(EARLY) * BLOCK, D)).reshape(len(EARLY), BLOCK, HD)
    for i, k in enumerate(EARLY):
        rbuf[(dp - k + NDP) % NDP] = got[i]
    for c in ex[len(EARLY) :]:
        c.wait_recv()
    for o in range(OUT):
        v = source_ref[o]
        local = gall[jnp.minimum(v, HELD - 1)]
        got = rbuf[jnp.maximum(v - HELD, 0)]
        ga_ref[pl.ds(o * BLOCK, BLOCK), :] = jnp.where(v < HELD, local, got)

    @pl.when(at_end)
    def _():
        for c in wh:
            c.wait_send()

    for c in [*wx, *hops, *shares, *pc, ca, cd, cb, *cy, *cz, *ex]:
        c.wait_send()


def on_device(held_acts, held_grads, layer_scale, out_weight, send_slots, out_source):
    order, wsel, ysel, zsel = (jnp.asarray(t) for t in tables())
    hbm = pl.BlockSpec(memory_space=pl.ANY)
    vmem = pl.BlockSpec(memory_space=pltpu.VMEM)
    smem = pl.BlockSpec(memory_space=pltpu.SMEM)
    dma = pltpu.SemaphoreType.DMA
    grad_acts, grad_weight = pl.pallas_call(
        kernel,
        out_shape=(
            jax.ShapeDtypeStruct((OUT * BLOCK, HD), BF16),
            jax.ShapeDtypeStruct((1, D), F32),
        ),
        in_specs=[hbm, hbm, hbm, vmem, vmem, smem, smem, vmem, vmem, vmem],
        out_specs=(vmem, vmem),
        scratch_shapes=[
            pltpu.VMEM((HD, HD), BF16),
            pltpu.VMEM((HELD * BLOCK, D), BF16),
            pltpu.VMEM((HD, HD), BF16),
            pltpu.VMEM((HELD + 1, BLOCK, D), BF16),
            pltpu.VMEM((NC, HD // NC, HD), BF16),
            pltpu.VMEM((NX, GROUP, D), F32),
            pltpu.VMEM((NX, GROUP, D), BF16),
            pltpu.VMEM((NX, GROUP, D), BF16),
            pltpu.VMEM((NX, NH, 16, 768), BF16),
            pltpu.VMEM((2, HD, 768), BF16),
            *[pltpu.VMEM((GROUP, D), BF16)] * 6,
            pltpu.VMEM((NY, 48, 384), BF16),
            pltpu.VMEM((NY, 48, 384), BF16),
            pltpu.VMEM((NZ, 16, 128), BF16),
            pltpu.VMEM((NZ, 16, 128), BF16),
            pltpu.VMEM((HELD + 1, BLOCK, HD), BF16),
            pltpu.VMEM((len(LATE), BLOCK, HD), BF16),
            pltpu.VMEM((NDP, BLOCK, HD), BF16),
            pltpu.VMEM((len(EARLY), BLOCK, D), BF16),
            pltpu.VMEM((len(EARLY), BLOCK, D), BF16),
            pltpu.VMEM((len(LATE), BLOCK, D), BF16),
            dma((3,)),
            dma((3,)), dma,
            dma((NX,)), dma((NX,)),
            dma((8 * PIECES,)), dma((8 * PIECES,)),
            dma((8,)), dma((8,)),
            dma((4,)), dma((4,)),
            dma((3,)), dma((3,)),
            dma((NY,)), dma((NY,)),
            dma((NZ,)), dma((NZ,)),
            dma((NDP,)), dma((NDP,)),
        ],
        compiler_params=pltpu.CompilerParams(
            collective_id=0, has_side_effects=True, vmem_limit_bytes=62 * 1024 * 1024
        ),
        cost_estimate=pl.CostEstimate(flops=5_000_000_000, bytes_accessed=8_000_000, transcendentals=0),
    )(
        held_acts,
        held_grads,
        order,
        layer_scale.reshape(1, D),
        out_weight,
        send_slots.reshape(NDP),
        out_source.reshape(OUT),
        wsel,
        ysel,
        zsel,
    )
    return grad_acts, grad_weight


def solution(mesh):
    in_specs = (
        P(("dp", "blk"), None),
        P(("dp", "blk"), None),
        P(),
        P("blk", None),
        P("dp", "blk", None),
        P("dp", "blk", None),
    )
    out_specs = (P(("dp", "blk"), None), P(("dp", "blk"), None))
    return jax.shard_map(
        on_device, mesh=mesh, in_specs=in_specs, out_specs=out_specs, check_vma=False
    )
```

```python
import math

import jax
import jax.numpy as jnp
import ml_dtypes
import numpy as np
from jax import lax
from jax.experimental import pallas as pl
from jax.experimental.pallas import tpu as pltpu
from jax.sharding import PartitionSpec as P

MESH = pl.DeviceIdType.MESH
BF16 = jnp.bfloat16
F32 = jnp.float32
BLOCK = 32
NX, NY, NH, NL, NC = 4, 8, 2, 6, 2
NZ = NH * NL
NDP = NL * NC
HELD, OUT = 23, 12
HD, D = 768, 1536
WROWS = 12
TOTAL_ROWS = NDP * NX * NY * NH * OUT * BLOCK
GROUP = HD // NC // NX
PIECES = 3
PIECE = GROUP // PIECES
EARLY = (6, 5, 7, 4, 8, 3, 9)
LATE = (2, 10, 1, 11)


def selection(rows, cols, pairs):
    m = np.zeros((rows, cols), np.float32)
    for r, c in pairs:
        m[r, c] = 1.0
    return m.astype(ml_dtypes.bfloat16)


def tables():
    grad_order = [
        (((c * NX + x) * NY + y) * NZ + h * NL + l, (l * NC + c) * 64 + (y * NX + x) * NH + h)
        for c in range(NC) for x in range(NX) for y in range(NY) for h in range(NH) for l in range(NL)
    ]
    weight_rows = [(WROWS * g + i, 16 * g + i) for g in range(NX * NH) for i in range(WROWS)]
    to_y = [((y * 4 + q) * NZ + z, (q * NY + y) * NZ + z) for q in range(4) for y in range(NY) for z in range(NZ)]
    to_z = [(z * 16 + 3 * q + j, (j * 4 + q) * NZ + z) for j in range(3) for q in range(4) for z in range(NZ)]
    return (
        selection(HD, HD, grad_order),
        selection(GROUP, 16 * NX * NH, weight_rows),
        selection(384, 384, to_y),
        selection(NZ * 16, 256, to_z),
    )


def matmul(a, b, dims=((1,), (0,))):
    return lax.dot_general(a, b, (dims, ((), ())), preferred_element_type=F32)


def kernel(
    acts_hbm, grads_hbm, order_hbm, scale_ref, w_ref, send_ref, source_ref, wsel_ref, ysel_ref, zsel_ref,
    ga_ref, gw_ref,
    acts, grads, order, scaled, acts_t, p_own, p_sib, p_rec, wbuf, wfull,
    xa, xd, xb, ra, rd, rb, ysend, yrecv, zsend, zrecv, gall, sbuf, rbuf, s_early, r_early, s_late,
    load_sem, wh_s, wh_r, wx_s, wx_r, ring_s, ring_r, sib_s, sib_r, pc_s, pc_r, x_s, x_r, y_s, y_r, z_s, z_r, e_s, e_r,
):
    dp = lax.axis_index("dp")
    blk = lax.axis_index("blk")
    zl, core = dp // 2, dp % 2
    y, x, zh = blk // 8, (blk // 2) % 4, blk % 2
    z = zh * NL + zl
    s = 1 - 2 * core

    def at_x(v):
        return (dp, y * 8 + v * 2 + zh)

    def at_y(v):
        return (dp, v * 8 + x * 2 + zh)

    def at_z(v):
        return ((v % NL) * 2 + core, y * 8 + x * 2 + v // NL)

    sibling = (dp + s, blk)

    def remote(src, dst, ss, rs, dev):
        return pltpu.make_async_remote_copy(
            src_ref=src, dst_ref=dst, send_sem=ss, recv_sem=rs, device_id=dev, device_id_type=MESH
        )

    loads = [
        pltpu.make_async_copy(grads_hbm, grads, load_sem.at[0]),
        pltpu.make_async_copy(acts_hbm, acts.at[pl.ds(0, HELD * BLOCK)], load_sem.at[1]),
        pltpu.make_async_copy(order_hbm, order, load_sem.at[2]),
    ]
    for c in loads:
        c.start()

    barrier = pltpu.get_barrier_semaphore()
    peers = [at_x((x + k) % NX) for k in range(1, NX)]
    peers += [at_y((y + k) % NY) for k in range(1, NY)]
    peers += [at_z((z + k) % NZ) for k in range(1, NZ)]
    peers += [((dp + k - core + 1 - core) % NDP, blk) for k in range(0, NDP, 2)]
    for dev in peers:
        pl.semaphore_signal(barrier, inc=1, device_id=dev, device_id_type=MESH)

    half = pl.ds(pl.multiple_of(core * 768, 768), 768)
    mine = w_ref[:, half].astype(F32)
    wbuf[x, zh] = jnp.concatenate([mine, jnp.zeros((16 - WROWS, 768), F32)], 0).astype(BF16)
    acts[pl.ds(HELD * BLOCK, BLOCK), :] = jnp.zeros((BLOCK, HD), BF16)
    scaled[HELD] = jnp.zeros((BLOCK, D), BF16)
    rbuf[dp] = jnp.zeros((BLOCK, HD), BF16)

    pl.semaphore_wait(barrier, len(peers))

    at_end = (zl == 0) | (zl == NL - 1)
    first = jnp.where(zl == 0, 3, 0)
    wh = [
        remote(wbuf.at[x, zh], wbuf.at[x, zh], wh_s.at[i], wh_r, at_z((1 - zh) * NL + first + i))
        for i in range(3)
    ]

    @pl.when(at_end)
    def _():
        for c in wh:
            c.start()

    def along_x(h, k, v, to):
        return remote(wbuf.at[v, h], wbuf.at[v, h], wx_s.at[k], wx_r.at[k], to)

    wx = [along_x(zh, k, x, at_x((x + k) % NX)) for k in range(1, NX)]
    for c in wx:
        c.start()

    kept = jnp.int32(0)
    for o in range(OUT):
        kept = kept + jnp.where(source_ref[o] < HELD, 1, 0)
    loads[0].wait()
    scale = scale_ref[...].reshape(1, D)

    def scale_block(j, _):
        used = j < kept
        for e in range(NDP):
            used = used | (send_ref[e] == j)
        factor = jnp.where(used, 1.0, 0.0).astype(F32)
        rows = pl.ds(pl.multiple_of(j * BLOCK, BLOCK), BLOCK)
        scaled[j] = (grads[rows, :].astype(F32) * (scale * factor)).astype(BF16)
        return 0

    lax.fori_loop(0, HELD, scale_block, 0)

    def chosen(k):
        return jnp.maximum(send_ref[(dp + k) % NDP], 0)

    ex = []
    for i, k in enumerate(EARLY):
        s_early[i] = scaled[chosen(k)]
        c = remote(s_early.at[i], r_early.at[i], e_s.at[k], e_r.at[k], ((dp + k) % NDP, blk))
        c.start()
        ex.append(c)

    remote(wbuf.at[x, 1 - zh], wbuf.at[x, 1 - zh], wh_s.at[0], wh_r, sibling).wait_recv()
    for k in range(1, NX):
        c = along_x(1 - zh, NX + k, x, at_x((x + k) % NX))
        c.start()
        wx.append(c)

    loads[1].wait()
    loads[2].wait()

    def transpose_tile(i, _):
        rows = pl.ds(pl.multiple_of(i * 384, 384), 384)
        acts_t[i] = matmul(order[rows, :], acts[...], ((1,), (1,))).astype(BF16)
        return 0

    lax.fori_loop(0, 2, transpose_tile, 0)

    def columns(n):
        return pl.ds(pl.multiple_of(n * 512, 512), 512)

    def rows_of(n):
        return scaled[:, :, columns(n)].reshape(HD, 512)

    def term_tile(n, _):
        t = matmul(acts_t[1 - core], rows_of(n)).astype(BF16)
        p_sib[:, :, columns(n)] = t.reshape(NX, GROUP, 512)
        return 0

    lax.fori_loop(0, 3, term_tile, 0)
    order_x = [(x + 2) % NX, (x + s + NX) % NX, (x - s + NX) % NX, x]
    pc = [remote(p_sib.at[v], p_rec.at[v], pc_s.at[k], pc_r.at[k], sibling) for k, v in enumerate(order_x)]
    for c in pc:
        c.start()

    def own_tile(n, _):
        p_own[:, :, columns(n)] = matmul(acts_t[core], rows_of(n)).reshape(NX, GROUP, 512)
        return 0

    lax.fori_loop(0, 3, own_tile, 0)

    right, left, far = (x + s + NX) % NX, (x - s + NX) % NX, (x + 2) % NX

    def from_sibling(k, v):
        remote(p_sib.at[v], p_rec.at[v], pc_s.at[k], pc_r.at[k], sibling).wait_recv()

    def term(v, h):
        return p_own[v, :, both[h]] + p_rec[v, :, both[h]].astype(F32)

    both = (pl.ds(0, 768), pl.ds(768, 768))

    def along_ring_x(src, dst, k, h, to):
        c = remote(src.at[h], dst.at[h], x_s.at[2 * k + h], x_r.at[2 * k + h], at_x(to))
        c.start()
        return c

    from_sibling(0, far)
    ca, cd, cb = [], [], []
    for h in range(2):
        xa[h] = term(far, h).astype(BF16)
        ca.append(along_ring_x(xa, ra, 0, h, right))
    from_sibling(1, left)
    for h in range(2):
        xd[h] = term(left, h).astype(BF16)
        cd.append(along_ring_x(xd, rd, 1, h, left))

    for k in range(1, NX):
        v = (x - k + NX) % NX
        along_x(zh, k, v, at_x(v)).wait_recv()
        along_x(1 - zh, NX + k, v, at_x(v)).wait_recv()

    def wchunk(c, v):
        return wfull.at[c, pl.ds(pl.multiple_of(v * GROUP, GROUP), GROUP)]

    def wpiece(v, p):
        return wfull.at[core, pl.ds(pl.multiple_of(v * GROUP + p * PIECE, PIECE), PIECE)]

    wfull[core, pl.ds(pl.multiple_of(y * GROUP, GROUP), GROUP), :] = matmul(
        wsel_ref[...], wbuf[...].reshape(16 * NX * NH, 768)
    ).astype(BF16)

    hops, shares = [], []

    def sign_of(way):
        return s if way == 0 else -s

    def hop(way, k, p):
        v = (y - sign_of(way) * k + 2 * NY) % NY
        sem = (way * 4 + k) * PIECES + p
        to = at_y((y + sign_of(way) + NY) % NY)
        c = remote(wpiece(v, p), wpiece(v, p), ring_s.at[sem], ring_r.at[sem], to)
        c.start()
        hops.append(c)

    def share(v):
        j = (v - y + NY) % NY
        c = remote(wchunk(core, v), wchunk(core, v), sib_s.at[j], sib_r.at[j], sibling)
        c.start()
        shares.append(c)

    for p in range(PIECES):
        hop(0, 0, p)
        hop(1, 0, p)
    share(y)

    def advance(k):
        for p in range(PIECES):
            for way, steps in ((0, 4), (1, 3)):
                if k < steps:
                    v = (y - sign_of(way) * (k + 1) + 2 * NY) % NY
                    sem = (way * 4 + k) * PIECES + p
                    remote(wpiece(v, p), wpiece(v, p), ring_s.at[sem], ring_r.at[sem], at_y(v)).wait_recv()
                    if k + 1 < steps:
                        hop(way, k + 1, p)
                    if p == PIECES - 1:
                        share(v)

    for i, k in enumerate(LATE):
        s_late[i] = scaled[chosen(k)]
    advance(0)
    from_sibling(2, right)
    for h in range(2):
        to_right = term(right, h)
        ca[h].wait_recv()
        xb[h] = (to_right + ra[h].astype(F32)).astype(BF16)
        cb.append(along_ring_x(xb, rb, 2, h, right))
    advance(1)
    advance(2)

    from_sibling(3, x)
    quarters = []
    for h in range(2):
        cd[h].wait_recv()
        cb[h].wait_recv()
        t = (term(x, h) + rd[h].astype(F32) + rb[h].astype(F32)).astype(BF16)
        quarters += [t[:, :384], t[:, 384:]]
    stacked = jnp.concatenate(quarters, 0)
    ysend[...] = matmul(ysel_ref[...], stacked).astype(BF16).reshape(NY, 48, 384)
    cy = []
    for k in range(1, NY):
        v = (y + k) % NY
        c = remote(ysend.at[v], yrecv.at[k], y_s.at[k], y_r.at[k], at_y(v))
        c.start()
        cy.append(c)

    advance(3)

    for j in range(NY):
        v = (y + j) % NY
        remote(wchunk(1 - core, v), wchunk(1 - core, v), sib_s.at[j], sib_r.at[j], sibling).wait_recv()

    def project(rows):
        t = matmul(rows[:, :768], wfull[0], ((1,), (1,)))
        t = t + matmul(rows[:, 768:], wfull[1], ((1,), (1,)))
        return t.astype(BF16)

    sbuf[...] = project(s_late[...].reshape(len(LATE) * BLOCK, D)).reshape(len(LATE), BLOCK, HD)
    for i, k in enumerate(LATE):
        c = remote(sbuf.at[i], rbuf.at[dp], e_s.at[k], e_r.at[k], ((dp + k) % NDP, blk))
        c.start()
        ex.append(c)

    def ga_tile(i, _):
        blocks = pl.ds(pl.multiple_of(i * 8, 8), 8)
        gall[blocks] = project(scaled[blocks].reshape(8 * BLOCK, D)).reshape(8, BLOCK, HD)
        return 0

    lax.fori_loop(0, 3, ga_tile, 0)

    total = ysend[y].astype(F32)
    for k in range(1, NY):
        cy[k - 1].wait_recv()
        total = total + yrecv[k].astype(F32)

    tz = total.astype(BF16)
    stacked = jnp.concatenate([tz[:, 128 * j : 128 * (j + 1)] for j in range(3)] + [jnp.zeros((112, 128), BF16)], 0)
    zsend[...] = matmul(zsel_ref[...], stacked).astype(BF16).reshape(NZ, 16, 128)
    cz = []
    for k in range(1, NZ):
        v = (z + k) % NZ
        c = remote(zsend.at[v], zrecv.at[k], z_s.at[k], z_r.at[k], at_z(v))
        c.start()
        cz.append(c)
    for c in ex[: len(EARLY)]:
        c.wait_recv()
    got = project(r_early[...].reshape(len(EARLY) * BLOCK, D)).reshape(len(EARLY), BLOCK, HD)
    for i, k in enumerate(EARLY):
        rbuf[(dp - k + NDP) % NDP] = got[i]
    total = zsend[z].astype(F32)
    for k in range(1, NZ):
        cz[k - 1].wait_recv()
        total = total + zrecv[k].astype(F32)
    for g in range(12):
        gw_ref[:, pl.ds(128 * g, 128)] = total[g : g + 1, :]

    for c in ex[len(EARLY) :]:
        c.wait_recv()
    for o in range(OUT):
        v = source_ref[o]
        local = gall[jnp.minimum(v, HELD - 1)]
        got = rbuf[jnp.maximum(v - HELD, 0)]
        ga_ref[pl.ds(o * BLOCK, BLOCK), :] = jnp.where(v < HELD, local, got)

    @pl.when(at_end)
    def _():
        for c in wh:
            c.wait_send()

    for c in [*wx, *hops, *shares, *pc, *ca, *cd, *cb, *cy, *cz, *ex]:
        c.wait_send()


def on_device(held_acts, held_grads, layer_scale, out_weight, send_slots, out_source):
    order, wsel, ysel, zsel = (jnp.asarray(t) for t in tables())
    hbm = pl.BlockSpec(memory_space=pl.ANY)
    vmem = pl.BlockSpec(memory_space=pltpu.VMEM)
    smem = pl.BlockSpec(memory_space=pltpu.SMEM)
    dma = pltpu.SemaphoreType.DMA
    grad_acts, grad_weight = pl.pallas_call(
        kernel,
        out_shape=(
            jax.ShapeDtypeStruct((OUT * BLOCK, HD), BF16),
            jax.ShapeDtypeStruct((1, D), F32),
        ),
        in_specs=[hbm, hbm, hbm, vmem, vmem, smem, smem, vmem, vmem, vmem],
        out_specs=(vmem, vmem),
        scratch_shapes=[
            pltpu.VMEM((HD, HD), BF16),
            pltpu.VMEM((HELD * BLOCK, D), BF16),
            pltpu.VMEM((HD, HD), BF16),
            pltpu.VMEM((HELD + 1, BLOCK, D), BF16),
            pltpu.VMEM((NC, HD // NC, HD), BF16),
            pltpu.VMEM((NX, GROUP, D), F32),
            pltpu.VMEM((NX, GROUP, D), BF16),
            pltpu.VMEM((NX, GROUP, D), BF16),
            pltpu.VMEM((NX, NH, 16, 768), BF16),
            pltpu.VMEM((2, HD, 768), BF16),
            *[pltpu.VMEM((2, GROUP, 768), BF16)] * 6,
            pltpu.VMEM((NY, 48, 384), BF16),
            pltpu.VMEM((NY, 48, 384), BF16),
            pltpu.VMEM((NZ, 16, 128), BF16),
            pltpu.VMEM((NZ, 16, 128), BF16),
            pltpu.VMEM((HELD + 1, BLOCK, HD), BF16),
            pltpu.VMEM((len(LATE), BLOCK, HD), BF16),
            pltpu.VMEM((NDP, BLOCK, HD), BF16),
            pltpu.VMEM((len(EARLY), BLOCK, D), BF16),
            pltpu.VMEM((len(EARLY), BLOCK, D), BF16),
            pltpu.VMEM((len(LATE), BLOCK, D), BF16),
            dma((3,)),
            dma((3,)), dma,
            dma((2 * NX,)), dma((2 * NX,)),
            dma((8 * PIECES,)), dma((8 * PIECES,)),
            dma((8,)), dma((8,)),
            dma((4,)), dma((4,)),
            dma((6,)), dma((6,)),
            dma((NY,)), dma((NY,)),
            dma((NZ,)), dma((NZ,)),
            dma((NDP,)), dma((NDP,)),
        ],
        compiler_params=pltpu.CompilerParams(
            collective_id=0, has_side_effects=True, vmem_limit_bytes=62 * 1024 * 1024
        ),
        cost_estimate=pl.CostEstimate(flops=5_000_000_000, bytes_accessed=8_000_000, transcendentals=0),
    )(
        held_acts,
        held_grads,
        order,
        layer_scale,
        out_weight,
        send_slots.reshape(NDP),
        out_source.reshape(OUT),
        wsel,
        ysel,
        zsel,
    )
    return grad_acts, grad_weight / math.sqrt(TOTAL_ROWS)


def solution(mesh):
    in_specs = (
        P(("dp", "blk"), None),
        P(("dp", "blk"), None),
        P(),
        P("blk", None),
        P("dp", "blk", None),
        P("dp", "blk", None),
    )
    out_specs = (P(("dp", "blk"), None), P(("dp", "blk"), None))
    return jax.shard_map(
        on_device, mesh=mesh, in_specs=in_specs, out_specs=out_specs, check_vma=False
    )
```

```python
import math

import jax
import jax.numpy as jnp
import ml_dtypes
import numpy as np
from jax import lax
from jax.experimental import pallas as pl
from jax.experimental.pallas import tpu as pltpu
from jax.sharding import PartitionSpec as P

MESH = pl.DeviceIdType.MESH
BF16 = jnp.bfloat16
F32 = jnp.float32
BLOCK = 32
NX, NY, NH, NL, NC = 4, 8, 2, 6, 2
NZ = NH * NL
NDP = NL * NC
HELD, OUT = 23, 12
HD, D = 768, 1536
WROWS = 12
TOTAL_ROWS = NDP * NX * NY * NH * OUT * BLOCK
GROUP = HD // NC // NX
PIECES = 3
PIECE = GROUP // PIECES
EARLY = (6, 5, 7, 4, 8, 3, 9)
LATE = (2, 10, 1, 11)


def selection(rows, cols, pairs):
    m = np.zeros((rows, cols), np.float32)
    for r, c in pairs:
        m[r, c] = 1.0
    return m.astype(ml_dtypes.bfloat16)


def tables():
    grad_order = [
        (((c * NX + x) * NY + y) * NZ + h * NL + l, (l * NC + c) * 64 + (y * NX + x) * NH + h)
        for c in range(NC) for x in range(NX) for y in range(NY) for h in range(NH) for l in range(NL)
    ]
    weight_rows = [(WROWS * g + i, 16 * g + i) for g in range(NX * NH) for i in range(WROWS)]
    to_y = [((y * 4 + q) * NZ + z, (q * NY + y) * NZ + z) for q in range(4) for y in range(NY) for z in range(NZ)]
    to_z = [(z * 16 + 3 * q + j, (j * 4 + q) * NZ + z) for j in range(3) for q in range(4) for z in range(NZ)]
    return (
        selection(HD, HD, grad_order),
        selection(GROUP, 16 * NX * NH, weight_rows),
        selection(384, 384, to_y),
        selection(NZ * 16, 256, to_z),
    )


def matmul(a, b, dims=((1,), (0,))):
    return lax.dot_general(a, b, (dims, ((), ())), preferred_element_type=F32)


def kernel(
    acts_hbm, grads_hbm, order_hbm, scale_ref, w_ref, send_ref, source_ref, wsel_ref, ysel_ref, zsel_ref,
    ga_ref, gw_ref,
    acts, grads, order, scaled, acts_t, p_own, p_sib, p_rec, wbuf, wfull,
    xa, xd, xb, ra, rd, rb, ysend, yrecv, zsend, zrecv, gall, sbuf, rbuf, s_early, r_early, s_late,
    load_sem, wh_s, wh_r, wx_s, wx_r, ring_s, ring_r, sib_s, sib_r, pc_s, pc_r, x_s, x_r, y_s, y_r, z_s, z_r, e_s, e_r,
):
    dp = lax.axis_index("dp")
    blk = lax.axis_index("blk")
    zl, core = dp // 2, dp % 2
    y, x, zh = blk // 8, (blk // 2) % 4, blk % 2
    z = zh * NL + zl
    s = 1 - 2 * core

    def at_x(v):
        return (dp, y * 8 + v * 2 + zh)

    def at_y(v):
        return (dp, v * 8 + x * 2 + zh)

    def at_z(v):
        return ((v % NL) * 2 + core, y * 8 + x * 2 + v // NL)

    sibling = (dp + s, blk)

    def remote(src, dst, ss, rs, dev):
        return pltpu.make_async_remote_copy(
            src_ref=src, dst_ref=dst, send_sem=ss, recv_sem=rs, device_id=dev, device_id_type=MESH
        )

    loads = [
        pltpu.make_async_copy(grads_hbm, grads, load_sem.at[0]),
        pltpu.make_async_copy(acts_hbm, acts.at[pl.ds(0, HELD * BLOCK)], load_sem.at[1]),
        pltpu.make_async_copy(order_hbm, order, load_sem.at[2]),
    ]
    for c in loads:
        c.start()

    barrier = pltpu.get_barrier_semaphore()
    peers = [at_x((x + k) % NX) for k in range(1, NX)]
    peers += [at_y((y + k) % NY) for k in range(1, NY)]
    peers += [at_z((z + k) % NZ) for k in range(1, NZ)]
    peers += [((dp + k - core + 1 - core) % NDP, blk) for k in range(0, NDP, 2)]
    for dev in peers:
        pl.semaphore_signal(barrier, inc=1, device_id=dev, device_id_type=MESH)

    half = pl.ds(pl.multiple_of(core * 768, 768), 768)
    mine = w_ref[:, half].astype(F32)
    wbuf[x, zh] = jnp.concatenate([mine, jnp.zeros((16 - WROWS, 768), F32)], 0).astype(BF16)
    acts[pl.ds(HELD * BLOCK, BLOCK), :] = jnp.zeros((BLOCK, HD), BF16)
    scaled[HELD] = jnp.zeros((BLOCK, D), BF16)
    rbuf[dp] = jnp.zeros((BLOCK, HD), BF16)

    pl.semaphore_wait(barrier, len(peers))

    at_end = (zl == 0) | (zl == NL - 1)
    first = jnp.where(zl == 0, 3, 0)
    wh = [
        remote(wbuf.at[x, zh], wbuf.at[x, zh], wh_s.at[i], wh_r, at_z((1 - zh) * NL + first + i))
        for i in range(3)
    ]

    @pl.when(at_end)
    def _():
        for c in wh:
            c.start()

    def along_x(h, k, v, to):
        return remote(wbuf.at[v, h], wbuf.at[v, h], wx_s.at[k], wx_r.at[k], to)

    wx = [along_x(zh, k, x, at_x((x + k) % NX)) for k in range(1, NX)]
    for c in wx:
        c.start()

    kept = jnp.int32(0)
    for o in range(OUT):
        kept = kept + jnp.where(source_ref[o] < HELD, 1, 0)
    loads[0].wait()
    scale = scale_ref[...].reshape(1, D)

    def scale_block(j, _):
        used = j < kept
        for e in range(NDP):
            used = used | (send_ref[e] == j)
        factor = jnp.where(used, 1.0, 0.0).astype(F32)
        rows = pl.ds(pl.multiple_of(j * BLOCK, BLOCK), BLOCK)
        scaled[j] = (grads[rows, :].astype(F32) * (scale * factor)).astype(BF16)
        return 0

    lax.fori_loop(0, HELD, scale_block, 0)

    def chosen(k):
        return jnp.maximum(send_ref[(dp + k) % NDP], 0)

    ex = []
    for i, k in enumerate(EARLY):
        s_early[i] = scaled[chosen(k)]
        c = remote(s_early.at[i], r_early.at[i], e_s.at[k], e_r.at[k], ((dp + k) % NDP, blk))
        c.start()
        ex.append(c)

    remote(wbuf.at[x, 1 - zh], wbuf.at[x, 1 - zh], wh_s.at[0], wh_r, sibling).wait_recv()
    for k in range(1, NX):
        c = along_x(1 - zh, NX + k, x, at_x((x + k) % NX))
        c.start()
        wx.append(c)

    loads[1].wait()
    loads[2].wait()

    def transpose_tile(i, _):
        rows = pl.ds(pl.multiple_of(i * 384, 384), 384)
        acts_t[i] = matmul(order[rows, :], acts[...], ((1,), (1,))).astype(BF16)
        return 0

    lax.fori_loop(0, 2, transpose_tile, 0)

    def columns(n):
        return pl.ds(pl.multiple_of(n * 512, 512), 512)

    def rows_of(n):
        return scaled[:, :, columns(n)].reshape(HD, 512)

    def term_tile(n, _):
        t = matmul(acts_t[1 - core], rows_of(n)).astype(BF16)
        p_sib[:, :, columns(n)] = t.reshape(NX, GROUP, 512)
        return 0

    lax.fori_loop(0, 3, term_tile, 0)
    order_x = [(x + 2) % NX, (x + s + NX) % NX, (x - s + NX) % NX, x]
    pc = [remote(p_sib.at[v], p_rec.at[v], pc_s.at[k], pc_r.at[k], sibling) for k, v in enumerate(order_x)]
    for c in pc:
        c.start()

    def own_tile(n, _):
        p_own[:, :, columns(n)] = matmul(acts_t[core], rows_of(n)).reshape(NX, GROUP, 512)
        return 0

    lax.fori_loop(0, 3, own_tile, 0)

    right, left, far = (x + s + NX) % NX, (x - s + NX) % NX, (x + 2) % NX

    def from_sibling(k, v):
        remote(p_sib.at[v], p_rec.at[v], pc_s.at[k], pc_r.at[k], sibling).wait_recv()

    def term(v, h):
        return p_own[v, :, both[h]] + p_rec[v, :, both[h]].astype(F32)

    both = (pl.ds(0, 768), pl.ds(768, 768))

    def along_ring_x(src, dst, k, h, to):
        c = remote(src.at[h], dst.at[h], x_s.at[2 * k + h], x_r.at[2 * k + h], at_x(to))
        c.start()
        return c

    from_sibling(0, far)
    ca, cd, cb = [], [], []
    for h in range(2):
        xa[h] = term(far, h).astype(BF16)
        ca.append(along_ring_x(xa, ra, 0, h, right))
    from_sibling(1, left)
    for h in range(2):
        xd[h] = term(left, h).astype(BF16)
        cd.append(along_ring_x(xd, rd, 1, h, left))

    for k in range(1, NX):
        v = (x - k + NX) % NX
        along_x(zh, k, v, at_x(v)).wait_recv()
        along_x(1 - zh, NX + k, v, at_x(v)).wait_recv()

    def wchunk(c, v):
        return wfull.at[c, pl.ds(pl.multiple_of(v * GROUP, GROUP), GROUP)]

    def wpiece(v, p):
        return wfull.at[core, pl.ds(pl.multiple_of(v * GROUP + p * PIECE, PIECE), PIECE)]

    wfull[core, pl.ds(pl.multiple_of(y * GROUP, GROUP), GROUP), :] = matmul(
        wsel_ref[...], wbuf[...].reshape(16 * NX * NH, 768)
    ).astype(BF16)

    hops, shares = [], []

    def sign_of(way):
        return s if way == 0 else -s

    def hop(way, k, p):
        v = (y - sign_of(way) * k + 2 * NY) % NY
        sem = (way * 4 + k) * PIECES + p
        to = at_y((y + sign_of(way) + NY) % NY)
        c = remote(wpiece(v, p), wpiece(v, p), ring_s.at[sem], ring_r.at[sem], to)
        c.start()
        hops.append(c)

    def share(v):
        j = (v - y + NY) % NY
        c = remote(wchunk(core, v), wchunk(core, v), sib_s.at[j], sib_r.at[j], sibling)
        c.start()
        shares.append(c)

    for p in range(PIECES):
        hop(0, 0, p)
        hop(1, 0, p)
    share(y)

    def advance(k):
        for p in range(PIECES):
            for way, steps in ((0, 4), (1, 3)):
                if k < steps:
                    v = (y - sign_of(way) * (k + 1) + 2 * NY) % NY
                    sem = (way * 4 + k) * PIECES + p
                    remote(wpiece(v, p), wpiece(v, p), ring_s.at[sem], ring_r.at[sem], at_y(v)).wait_recv()
                    if k + 1 < steps:
                        hop(way, k + 1, p)
                    if p == PIECES - 1:
                        share(v)

    for i, k in enumerate(LATE):
        s_late[i] = scaled[chosen(k)]
    advance(0)
    from_sibling(2, right)
    for h in range(2):
        to_right = term(right, h)
        ca[h].wait_recv()
        xb[h] = (to_right + ra[h].astype(F32)).astype(BF16)
        cb.append(along_ring_x(xb, rb, 2, h, right))
    advance(1)
    advance(2)

    from_sibling(3, x)
    quarters = []
    for h in range(2):
        cd[h].wait_recv()
        cb[h].wait_recv()
        t = (term(x, h) + rd[h].astype(F32) + rb[h].astype(F32)).astype(BF16)
        quarters += [t[:, :384], t[:, 384:]]
    stacked = jnp.concatenate(quarters, 0)
    ysend[...] = matmul(ysel_ref[...], stacked).astype(BF16).reshape(NY, 48, 384)
    cy = []
    for k in range(1, NY):
        v = (y + k) % NY
        c = remote(ysend.at[v], yrecv.at[k], y_s.at[k], y_r.at[k], at_y(v))
        c.start()
        cy.append(c)

    advance(3)

    for j in range(NY):
        v = (y + j) % NY
        remote(wchunk(1 - core, v), wchunk(1 - core, v), sib_s.at[j], sib_r.at[j], sibling).wait_recv()

    def project(rows):
        t = matmul(rows[:, :768], wfull[0], ((1,), (1,)))
        t = t + matmul(rows[:, 768:], wfull[1], ((1,), (1,)))
        return t.astype(BF16)

    sbuf[...] = project(s_late[...].reshape(len(LATE) * BLOCK, D)).reshape(len(LATE), BLOCK, HD)
    for i, k in enumerate(LATE):
        c = remote(sbuf.at[i], rbuf.at[dp], e_s.at[k], e_r.at[k], ((dp + k) % NDP, blk))
        c.start()
        ex.append(c)


    total = ysend[y].astype(F32)
    for k in range(1, NY):
        cy[k - 1].wait_recv()
        total = total + yrecv[k].astype(F32)

    tz = total.astype(BF16)
    stacked = jnp.concatenate([tz[:, 128 * j : 128 * (j + 1)] for j in range(3)] + [jnp.zeros((112, 128), BF16)], 0)
    zsend[...] = matmul(zsel_ref[...], stacked).astype(BF16).reshape(NZ, 16, 128)
    cz = []
    for k in range(1, NZ):
        v = (z + k) % NZ
        c = remote(zsend.at[v], zrecv.at[k], z_s.at[k], z_r.at[k], at_z(v))
        c.start()
        cz.append(c)
    def ga_tile(i, _):
        blocks = pl.ds(pl.multiple_of(i * 8, 8), 8)
        gall[blocks] = project(scaled[blocks].reshape(8 * BLOCK, D)).reshape(8, BLOCK, HD)
        return 0

    lax.fori_loop(0, 3, ga_tile, 0)

    for c in ex[: len(EARLY)]:
        c.wait_recv()
    got = project(r_early[...].reshape(len(EARLY) * BLOCK, D)).reshape(len(EARLY), BLOCK, HD)
    for i, k in enumerate(EARLY):
        rbuf[(dp - k + NDP) % NDP] = got[i]
    total = zsend[z].astype(F32)
    for k in range(1, NZ):
        cz[k - 1].wait_recv()
        total = total + zrecv[k].astype(F32)
    for g in range(12):
        gw_ref[:, pl.ds(128 * g, 128)] = total[g : g + 1, :]

    for c in ex[len(EARLY) :]:
        c.wait_recv()
    for o in range(OUT):
        v = source_ref[o]
        local = gall[jnp.minimum(v, HELD - 1)]
        got = rbuf[jnp.maximum(v - HELD, 0)]
        ga_ref[pl.ds(o * BLOCK, BLOCK), :] = jnp.where(v < HELD, local, got)

    @pl.when(at_end)
    def _():
        for c in wh:
            c.wait_send()

    for c in [*wx, *hops, *shares, *pc, *ca, *cd, *cb, *cy, *cz, *ex]:
        c.wait_send()


def on_device(held_acts, held_grads, layer_scale, out_weight, send_slots, out_source):
    order, wsel, ysel, zsel = (jnp.asarray(t) for t in tables())
    hbm = pl.BlockSpec(memory_space=pl.ANY)
    vmem = pl.BlockSpec(memory_space=pltpu.VMEM)
    smem = pl.BlockSpec(memory_space=pltpu.SMEM)
    dma = pltpu.SemaphoreType.DMA
    grad_acts, grad_weight = pl.pallas_call(
        kernel,
        out_shape=(
            jax.ShapeDtypeStruct((OUT * BLOCK, HD), BF16),
            jax.ShapeDtypeStruct((1, D), F32),
        ),
        in_specs=[hbm, hbm, hbm, vmem, vmem, smem, smem, vmem, vmem, vmem],
        out_specs=(vmem, vmem),
        scratch_shapes=[
            pltpu.VMEM((HD, HD), BF16),
            pltpu.VMEM((HELD * BLOCK, D), BF16),
            pltpu.VMEM((HD, HD), BF16),
            pltpu.VMEM((HELD + 1, BLOCK, D), BF16),
            pltpu.VMEM((NC, HD // NC, HD), BF16),
            pltpu.VMEM((NX, GROUP, D), F32),
            pltpu.VMEM((NX, GROUP, D), BF16),
            pltpu.VMEM((NX, GROUP, D), BF16),
            pltpu.VMEM((NX, NH, 16, 768), BF16),
            pltpu.VMEM((2, HD, 768), BF16),
            *[pltpu.VMEM((2, GROUP, 768), BF16)] * 6,
            pltpu.VMEM((NY, 48, 384), BF16),
            pltpu.VMEM((NY, 48, 384), BF16),
            pltpu.VMEM((NZ, 16, 128), BF16),
            pltpu.VMEM((NZ, 16, 128), BF16),
            pltpu.VMEM((HELD + 1, BLOCK, HD), BF16),
            pltpu.VMEM((len(LATE), BLOCK, HD), BF16),
            pltpu.VMEM((NDP, BLOCK, HD), BF16),
            pltpu.VMEM((len(EARLY), BLOCK, D), BF16),
            pltpu.VMEM((len(EARLY), BLOCK, D), BF16),
            pltpu.VMEM((len(LATE), BLOCK, D), BF16),
            dma((3,)),
            dma((3,)), dma,
            dma((2 * NX,)), dma((2 * NX,)),
            dma((8 * PIECES,)), dma((8 * PIECES,)),
            dma((8,)), dma((8,)),
            dma((4,)), dma((4,)),
            dma((6,)), dma((6,)),
            dma((NY,)), dma((NY,)),
            dma((NZ,)), dma((NZ,)),
            dma((NDP,)), dma((NDP,)),
        ],
        compiler_params=pltpu.CompilerParams(
            collective_id=0, has_side_effects=True, vmem_limit_bytes=62 * 1024 * 1024
        ),
        cost_estimate=pl.CostEstimate(flops=5_000_000_000, bytes_accessed=8_000_000, transcendentals=0),
    )(
        held_acts,
        held_grads,
        order,
        layer_scale,
        out_weight,
        send_slots.reshape(NDP),
        out_source.reshape(OUT),
        wsel,
        ysel,
        zsel,
    )
    return grad_acts, grad_weight / math.sqrt(TOTAL_ROWS)


def solution(mesh):
    in_specs = (
        P(("dp", "blk"), None),
        P(("dp", "blk"), None),
        P(),
        P("blk", None),
        P("dp", "blk", None),
        P("dp", "blk", None),
    )
    out_specs = (P(("dp", "blk"), None), P(("dp", "blk"), None))
    return jax.shard_map(
        on_device, mesh=mesh, in_specs=in_specs, out_specs=out_specs, check_vma=False
    )
```
